32 devices in a mesh: grp: 2 (over y), ia: 4 (over x, core), ja: 4 (over z).
Axes of the slice: x: 2, y: 2, z: 4, core: 2. Of those that a mesh axis runs over, the one named last changes fastest.
Arguments:
- amplitudes: float32 [16, 8, 160, 160], P(('grp', 'ia'), 'ja'), parts along dimension 0, may hold values from -3 to 3
- integrals: float32 [16, 8, 160, 160], P(('grp', 'ia'), 'ja'), parts along dimension 0, may hold values from -6 to 6
- row_intersection: float32 [16, 8, 8, 160, 160], P(('grp', 'ia'), 'ja'), parts along dimension 0, as said below
- column_intersection: float32 [16, 8, 8, 160, 160], P(('grp', 'ia'), 'ja'), parts along dimension 0, as said below
- row_tiles: int32 [16, 8], P(('grp', 'ia')), parts along dimension 0, may hold values from 0 to 7, as said below
- row_coupling: float32 [16, 8], P(('grp', 'ia')), parts along dimension 0, may hold values from 0.02 to 0.12
- row_counts: int32 [16], P(('grp', 'ia')), parts along dimension 0, may hold values from 1 to 8, as said below
- column_tiles: int32 [16, 8], P(('grp', 'ja')), parts along dimension 0, may hold values from 0 to 7, as said below
- column_coupling: float32 [16, 8], P(('grp', 'ja')), parts along dimension 0, may hold values from 0.02 to 0.12
- column_counts: int32 [16], P(('grp', 'ja')), parts along dimension 0, may hold values from 1 to 8, as said below
- virtual_energy: float32 [16, 8, 160], P(('grp', 'ia'), 'ja'), parts along dimension 0, may hold values from 0.5 to 3
- first_energy: float32 [16], P(('grp', 'ia')), parts along dimension 0, may hold values from -1.5 to -0.3
- second_energy: float32 [16], P(('grp', 'ja')), parts along dimension 0, may hold values from -1.5 to -0.3
Outputs:
- new_amplitudes: float32 [16, 8, 160, 160], P(('grp', 'ia'), 'ja'), parts along dimension 0
- last_residual: float32 [16, 8, 160, 160], P(('grp', 'ia'), 'ja'), parts along dimension 0
The draws below stay inside these ranges and needn't reach their ends.
There are 2 independent parts, one for each index of `grp`. The reference program is written for one: setup_inputs(seed, part) draws one part's arguments, and reference() takes and returns one part's arrays. A program takes and returns all parts, laid end to end along the dimension named above; each array names one. Nothing has to cross between parts.
Inputs may be any that keep to these rules, and one draw needn't show every extreme that they name: `row_tiles`: each row holds 8 different first-fragment orbitals. `column_tiles`: each row holds 8 different second-fragment orbitals. `row_counts`: some orbital has all 8 slots live. `column_counts`: some orbital has all 8 slots live. `row_intersection`: identity plus an independent perturbation of full rank. `column_intersection`: identity plus an independent perturbation of full rank.
All inputs are finite; a program needn't handle non-finite values.
Results may differ from the reference program's by a relative error of at most 0.00017.
Values sent between devices are 32-bit elements; how exact they have to be, the bound alone decides.
A program may use at most 128 MiB of HBM per device.

```python
import math
import jax
import jax.numpy as jnp
from jax import lax

P_SIZE = 160
ITERS = 2
NI = 8
NJ = 8
KL = 8


def intersection_draw(key):
    shape = (NI, NJ, KL, P_SIZE, P_SIZE)
    spread = 0.4 / P_SIZE ** 0.5
    noise = jax.random.normal(key, shape, jnp.float32) * spread
    return noise + jnp.eye(P_SIZE, dtype=jnp.float32)


def draw_row_intersection(key, part):
    return intersection_draw(jax.random.fold_in(key, 11))


def draw_column_intersection(key, part):
    return intersection_draw(jax.random.fold_in(key, 13))


def tile_lists(key, total):
    keys = jax.random.split(key, total)
    return jax.vmap(lambda single: jax.random.permutation(single, total)[:KL])(keys).astype(jnp.int32)


def draw_row_tiles(key, part):
    return tile_lists(jax.random.fold_in(key, 21), NI)


def draw_column_tiles(key, part):
    return tile_lists(jax.random.fold_in(key, 23), NJ)


def live_counts(key, total):
    first, second = jax.random.split(key)
    counts = jax.random.randint(first, (total,), 1, KL + 1, dtype=jnp.int32)
    where = jax.random.randint(second, (), 0, total, dtype=jnp.int32)
    return counts.at[where].set(KL)


def draw_row_counts(key, part):
    return live_counts(jax.random.fold_in(key, 31), NI)


def draw_column_counts(key, part):
    return live_counts(jax.random.fold_in(key, 33), NJ)


def shard_levels(stream_key, extent, cuts, least, top_value):
    def one(dim, shards_of):
        draws = jax.random.uniform(jax.random.fold_in(jax.random.fold_in(stream_key, 6), dim), (shards_of,), jnp.float32, least / len(cuts), top_value / len(cuts))
        return jnp.repeat(jnp.exp(draws), extent[dim] // shards_of).reshape((-1,) + (1,) * (len(extent) - dim - 1))

    factor_of = one(*cuts[0])
    for cut in cuts[1:]:
        factor_of = factor_of * one(*cut)
    return factor_of


def scatter_about(stream_key, extent, scale, bound, pieces=(), kind=jnp.bfloat16):
    entries = jax.random.normal(stream_key, extent, jnp.float32) * scale
    if len(pieces) > 0:
        entries = shard_levels(stream_key, extent, pieces, -0.22, 0.18) * entries
    return jnp.clip(entries, min=-bound, max=bound).astype(kind)


def setup_inputs(seed: int = 0, part: int = 0) -> dict:
    arg_keys = jax.random.split(jax.random.key(seed), 14)
    own_keys = jax.random.split(jax.random.fold_in(arg_keys[13], part), 14)
    amplitudes = scatter_about(own_keys[0], (NI, NJ, P_SIZE, P_SIZE), 0.5, 3.0, ((0, 4), (1, 4)), jnp.float32)
    integrals = scatter_about(own_keys[1], (NI, NJ, P_SIZE, P_SIZE), 1.0, 6.0, ((0, 4), (1, 4)), jnp.float32)
    row_intersection = draw_row_intersection(jax.random.fold_in(jax.random.fold_in(arg_keys[13], part), 71), part)
    column_intersection = draw_column_intersection(jax.random.fold_in(jax.random.fold_in(arg_keys[13], part), 71), part)
    row_tiles = draw_row_tiles(jax.random.fold_in(jax.random.fold_in(arg_keys[13], part), 71), part)
    row_coupling = jnp.clip(jnp.exp(math.log(0.12) - 1.7917595 * jax.random.uniform(own_keys[5], (NI, KL), jnp.float32) ** shard_levels(own_keys[5], (NI, KL), ((0, 4),), -0.2, 0.2)), 0.02, 0.12)
    row_counts = draw_row_counts(jax.random.fold_in(jax.random.fold_in(arg_keys[13], part), 71), part)
    column_tiles = draw_column_tiles(jax.random.fold_in(jax.random.fold_in(arg_keys[13], part), 71), part)
    column_coupling = jnp.clip(jnp.exp(math.log(0.12) - 1.7917595 * jax.random.uniform(own_keys[8], (NJ, KL), jnp.float32) ** shard_levels(own_keys[8], (NJ, KL), ((0, 4),), -0.2, 0.2)), 0.02, 0.12)
    column_counts = draw_column_counts(jax.random.fold_in(jax.random.fold_in(arg_keys[13], part), 71), part)
    virtual_energy = jnp.clip(0.5 + 2.5 * jax.random.uniform(own_keys[10], (NI, NJ, P_SIZE), jnp.float32) ** shard_levels(own_keys[10], (NI, NJ, P_SIZE), ((0, 4), (1, 4)), -0.2, 0.2), 0.5, 3.0)
    first_energy = jnp.clip(-1.5 + 1.2 * jax.random.uniform(own_keys[11], (NI,), jnp.float32) ** shard_levels(own_keys[11], (NI,), ((0, 4),), -0.2, 0.2), -1.5, -0.3)
    second_energy = jnp.clip(-1.5 + 1.2 * jax.random.uniform(own_keys[12], (NJ,), jnp.float32) ** shard_levels(own_keys[12], (NJ,), ((0, 4),), -0.2, 0.2), -1.5, -0.3)
    return dict(amplitudes=amplitudes, integrals=integrals, row_intersection=row_intersection, column_intersection=column_intersection, row_tiles=row_tiles, row_coupling=row_coupling, row_counts=row_counts, column_tiles=column_tiles, column_coupling=column_coupling, column_counts=column_counts, virtual_energy=virtual_energy, first_energy=first_energy, second_energy=second_energy)


def sandwich(intersection, block):
    left = jnp.matmul(intersection, block, precision=lax.Precision.HIGHEST)
    return jnp.matmul(left, jnp.swapaxes(intersection, -1, -2), precision=lax.Precision.HIGHEST)


def reference(amplitudes, integrals, row_intersection, column_intersection, row_tiles, row_coupling, row_counts, column_tiles, column_coupling, column_counts, virtual_energy, first_energy, second_energy):
    denom = virtual_energy[:, :, :, None] + virtual_energy[:, :, None, :] - first_energy[:, None, None, None] - second_energy[None, :, None, None]
    slot_index = jnp.arange(row_tiles.shape[1], dtype=jnp.int32)
    row_weight = row_coupling * (slot_index[None, :] < row_counts[:, None]).astype(row_coupling.dtype)
    column_weight = column_coupling * (slot_index[None, :] < column_counts[:, None]).astype(column_coupling.dtype)
    current = amplitudes
    residual = jnp.zeros_like(amplitudes)
    for iteration in range(ITERS):
        def row_part(packed):
            tiles, weight, intersection = packed
            chosen = jnp.swapaxes(current[tiles], 0, 1)
            product = sandwich(intersection, chosen)
            return jnp.einsum('l,jlab->jab', weight, product, precision=lax.Precision.HIGHEST)

        def column_part(packed):
            own_row, intersection = packed
            chosen = own_row[column_tiles]
            product = sandwich(intersection, chosen)
            return jnp.einsum('jl,jlab->jab', column_weight, product, precision=lax.Precision.HIGHEST)

        row_term = lax.map(row_part, (row_tiles, row_weight, row_intersection))
        column_term = lax.map(column_part, (current, column_intersection))
        residual = integrals + denom * current - row_term - column_term
        current = current - residual / denom
    return current, residual
```

```python
import functools

import jax
import jax.numpy as jnp
from jax import lax
from jax.experimental import pallas as pl
from jax.experimental.pallas import tpu as pltpu
from jax.sharding import PartitionSpec as P

ITERS = 2
LANES = 128
MESH = pl.DeviceIdType.MESH
BF16 = jnp.bfloat16
F32 = jnp.float32


def split(x):
    high = x.astype(BF16)
    return high, (x - high.astype(F32)).astype(BF16)


def dot(a, b, b_side):
    return lax.dot_general(a, b, (((1,), (b_side,)), ((), ())), preferred_element_type=F32)


def product3(a, b_high, b_low, b_side):
    rows = a.shape[0]
    a_high, a_low = split(a)
    both = dot(jnp.concatenate([a_high, a_low], axis=0), b_high, b_side)
    return both[:rows] + both[rows:] + dot(a_high, b_low, b_side)


class Wire:
    def __init__(self, tiles, size):
        self.tiles, self.size = tiles, size
        self.full = size // LANES
        self.rest = size % LANES
        self.per = LANES // self.rest if self.rest else tiles
        self.shared = -(-tiles // self.per) if self.rest else 0
        self.planes = tiles * self.full + self.shared
        half = tiles // 2 * self.full
        self.chunks = ((0, half), (half, self.planes)) if half else ((0, self.planes),)


def events_of(ni, nj, nia, nja):
    cores = 2 if nia % 2 == 0 else 1
    places = nia // cores
    groups = [[("row", "own", 0, 0), ("col", "own", 0, 0)]]
    if cores == 2:
        groups.append([("row", "core", 0, 1)])
    for t in range(1, max(places, nja)):
        group = []
        if t < nja:
            group += [("col", "up", t, 0), ("col", "down", t, 0)]
        if t < places:
            group.append(("row", "place", t, 0))
            if cores == 2:
                group.append(("row", "core", t, 1))
        groups.append(group)
    return cores, places, groups


def kernel(
    nia, nja, wire,
    amp, integ, row_tiles, row_coup, row_counts, col_tiles, col_coup, col_counts, virt, first, second,
    row_s, col_s,
    new_amp, last_res,
    s_all, buf, cur, acc, den, t_high, t_low, slot_tab, weight_tab, load_sem, send_sem, recv_sem,
):
    ni, nj, size, _ = amp.shape
    pairs = ni * nj
    slots = row_tiles.shape[1]
    cores, places, groups = events_of(ni, nj, nia, nja)
    me_a, me_z = lax.axis_index("ia"), lax.axis_index("ja")
    place, core = me_a // cores, me_a % cores
    chunks = wire.chunks
    own_norb = (nia * ni, nja * nj)

    loads = [
        pltpu.make_async_copy(row_s, s_all.at[0], load_sem.at[0]),
        pltpu.make_async_copy(col_s, s_all.at[1], load_sem.at[1]),
    ]
    for load in loads:
        load.start()

    def sibling():
        return {"ia": place * cores + (core + 1) % cores}

    def placed(step):
        return {"ia": ((place + step) % places) * cores + core}

    has_up, has_down = me_z < nja - 1, me_z > 0

    barrier = pltpu.get_barrier_semaphore()

    def greet(device):
        pl.semaphore_signal(barrier, inc=1, device_id=device, device_id_type=MESH)

    if cores == 2:
        greet(sibling())
    for step in range(1, places):
        greet(placed(step))
    if nja > 1:
        @pl.when(has_up)
        def _():
            greet({"ja": me_z + 1})

        @pl.when(has_down)
        def _():
            greet({"ja": me_z - 1})

    flat = [event for group in groups for event in group]
    info = []
    next_buffer = 1
    where = {}
    for event in flat:
        kind, how, step, flip = event
        if how == "own":
            index, here = 0, jnp.bool_(True)
        else:
            index, here = next_buffer, jnp.bool_(True)
            next_buffer += 1
        if how == "up":
            source, here = me_z - step, me_z - step >= 0
        elif how == "down":
            source, here = me_z + step, me_z + step < nja
        elif kind == "col":
            source = me_z
        else:
            source = ((place + places - step) % places) * cores + (core + flip) % cores
        where[(how, step)] = index
        info.append((0 if kind == "row" else 1, index, source, here))

    def copy(it, number, source_index, target_index, chunk, device):
        low, high = chunks[chunk]
        return pltpu.make_async_remote_copy(
            src_ref=buf.at[it, source_index, pl.ds(low, high - low)],
            dst_ref=buf.at[it, target_index, pl.ds(low, high - low)],
            send_sem=send_sem.at[it, number * len(chunks) + chunk],
            recv_sem=recv_sem.at[it, target_index * len(chunks) + chunk],
            device_id=device,
            device_id_type=MESH,
        )

    sends = []
    if nja > 1:
        for t in range(0, nja - 1):
            source_up = where[("up", t)] if t else 0
            source_down = where[("down", t)] if t else 0
            sends.append((("up", t) if t else ("own", 0), source_up, where[("up", t + 1)], {"ja": me_z + 1}, has_up & (me_z - t >= 0)))
            sends.append((("down", t) if t else ("own", 0), source_down, where[("down", t + 1)], {"ja": me_z - 1}, has_down & (me_z + t < nja)))
    for t in range(1, places):
        sends.append((("own", 0), 0, where[("place", t)], placed(t), None))
    if cores == 2:
        sends.append((("own", 0), 0, where[("core", 0)], sibling(), None))
        for t in range(1, places):
            sends.append((("place", t), where[("place", t)], where[("core", t)], sibling(), None))
    sends = [(number,) + send for number, send in enumerate(sends)]

    def guarded(condition, act):
        if condition is None:
            act()
        else:
            pl.when(condition)(act)

    def send_after(key, it, chunk):
        for number, after, source_index, target_index, device, condition in sends:
            if after == key:
                guarded(
                    condition,
                    lambda: copy(it, number, source_index, target_index, chunk, device).start(),
                )

    def wait_chunk(it, index, chunk):
        copy(it, 0, index, index, chunk, {"ja": me_z, "ia": me_a}).wait_recv()

    def pack(it, p):
        tile = cur[p]
        for f in range(wire.full):
            buf[it, 0, p * wire.full + f] = tile[:, f * LANES:(f + 1) * LANES]

    def pack_shared(it):
        for plane in range(wire.shared):
            some = [
                cur[p, :, wire.full * LANES:]
                for p in range(plane * wire.per, min(pairs, (plane + 1) * wire.per))
            ]
            room = LANES - len(some) * wire.rest
            if room:
                some.append(jnp.zeros((size, room), F32))
            buf[it, 0, pairs * wire.full + plane] = jnp.concatenate(some, axis=1)

    def send_own(it):
        half = pairs // 2 if len(chunks) == 2 else pairs
        for p in range(half):
            pack(it, p)
        if len(chunks) == 2:
            send_after(("own", 0), it, 0)
            for p in range(half, pairs):
                pack(it, p)
        pack_shared(it)
        send_after(("own", 0), it, len(chunks) - 1)

    for p in range(pairs):
        cur[p] = amp[p // nj, p % nj]
    greeted = (1 if cores == 2 else 0) + places - 1
    if nja > 1:
        greeted = greeted + has_up.astype(jnp.int32) + has_down.astype(jnp.int32)
    pl.semaphore_wait(barrier, greeted)
    send_own(0)

    for kind, (tiles, coup, counts, count) in enumerate(
        ((row_tiles, row_coup, row_counts, ni), (col_tiles, col_coup, col_counts, nj))
    ):
        for a in range(count):
            def fill(k, carry, kind=kind, tiles=tiles, coup=coup, counts=counts, a=a):
                slot, weight = jnp.int32(0), F32(0)
                live = counts[a]
                for l in range(slots):
                    match = tiles[a, l] == k
                    slot = jnp.where(match, jnp.int32(l), slot)
                    weight = jnp.where(match & (l < live), coup[a, l], weight)
                slot_tab[kind, a, k] = slot
                weight_tab[kind, a, k] = weight
                return carry

            lax.fori_loop(0, own_norb[kind], fill, 0)

    rows_of = lax.broadcasted_iota(jnp.int32, (size, size), 0)
    columns_of = lax.broadcasted_iota(jnp.int32, (size, size), 1)
    for p in range(pairs):
        i, j = p // nj, p % nj
        across = virt[i, j:j + 1, :]
        down = jnp.sum(jnp.where(rows_of == columns_of, across, 0.0), axis=1, keepdims=True)
        den[p] = down + across - first[i] - second[j]
        acc[p] = jnp.zeros((size, size), F32)

    for load in loads:
        load.wait()

    def pick(e, values):
        out = values[0]
        for index in range(1, len(values)):
            out = jnp.where(e == index, values[index], out)
        return out

    def one_event(it, e):
        start = 0
        for group in groups:
            arriving = [event for event in group if event[1] != "own"]

            def take(group=arriving, start=start):
                for chunk in range(len(chunks)):
                    for kind, how, step, flip in group:
                        if how == "core" and step:
                            continue
                        here = info[flat.index((kind, how, step, flip))][3]

                        def arrive(how=how, step=step, chunk=chunk):
                            wait_chunk(it, where[(how, step)], chunk)
                            send_after((how, step), it, chunk)

                        guarded(here if how in ("up", "down") else None, arrive)

            if arriving:
                pl.when(e == start)(take)
                for kind, how, step, flip in arriving:
                    if how == "core" and step:
                        @pl.when(e == flat.index((kind, how, step, flip)))
                        def _(step=step):
                            for chunk in range(len(chunks)):
                                wait_chunk(it, where[("core", step)], chunk)
            start += len(group)

        kind = pick(e, [jnp.int32(x[0]) for x in info])
        index = pick(e, [jnp.int32(x[1]) for x in info])
        source = pick(e, [x[2] for x in info])
        here = pick(e, [x[3].astype(jnp.int32) for x in info]) > 0

        @pl.when(here)
        def _():
            for p in range(pairs):
                for f in range(wire.full):
                    lanes = slice(f * LANES, (f + 1) * LANES)
                    t_high[p, :, lanes], t_low[p, :, lanes] = split(buf[it, index, p * wire.full + f])
                if wire.rest:
                    part = buf[it, index, pairs * wire.full + p // wire.per]
                    offset = p % wire.per * wire.rest
                    if offset:
                        part = pltpu.roll(part, LANES - offset, 1)
                    lanes = slice(wire.full * LANES, size)
                    t_high[p, :, lanes], t_low[p, :, lanes] = split(part[:, :wire.rest])

            is_row = kind == 0

            def one_orbital(inner, carry):
                orbital = source * jnp.where(is_row, ni, nj) + inner
                for p in range(pairs):
                    i, j = p // nj, p % nj
                    mine = jnp.where(is_row, i, j)
                    slot = slot_tab[kind, mine, orbital]
                    weight = weight_tab[kind, mine, orbital]
                    tile = jnp.where(is_row, inner * nj + j, i * nj + inner)
                    s = s_all[kind, i, j, slot]
                    s_high, s_low = split(s)
                    x = dot(jnp.concatenate([s_high, s_low], axis=0), t_high[tile], 0)
                    x = x[:size] + x[size:] + dot(s_high, t_low[tile], 0)
                    acc[p] += product3(x * weight, s_high, s_low, 1)
                return carry

            lax.fori_loop(0, ni if ni == nj else jnp.where(is_row, ni, nj), one_orbital, 0)

    def one_iteration(it, carry):
        def step(e, inner):
            one_event(it, e)
            return inner

        lax.fori_loop(0, len(flat), step, 0)

        for p in range(pairs):
            i, j = p // nj, p % nj
            residual = integ[i, j] + den[p] * cur[p] - acc[p]
            last_res[i, j] = residual
            cur[p] = cur[p] - residual / den[p]
            acc[p] = jnp.zeros((size, size), F32)

        @pl.when(it < ITERS - 1)
        def _():
            send_own(it + 1)

        return carry

    lax.fori_loop(0, ITERS, one_iteration, 0)
    for p in range(pairs):
        new_amp[p // nj, p % nj] = cur[p]

    def drain(it, carry):
        for number, after, source_index, target_index, device, condition in sends:
            for chunk in range(len(chunks)):
                guarded(
                    condition,
                    lambda: copy(it, number, source_index, target_index, chunk, device).wait_send(),
                )
        return carry

    lax.fori_loop(0, ITERS, drain, 0)


def local(
    nia, nja,
    amplitudes, integrals, row_intersection, column_intersection, row_tiles, row_coupling, row_counts,
    column_tiles, column_coupling, column_counts, virtual_energy, first_energy, second_energy,
):
    ni, nj, size, _ = amplitudes.shape
    slots = row_tiles.shape[1]
    pairs = ni * nj
    wire = Wire(pairs, size)
    cores, places, groups = events_of(ni, nj, nia, nja)
    buffers = sum(len(group) for group in groups) - 1
    number_sends = 2 * (nja - 1) + (places - 1) + (places if cores == 2 else 0)
    norb = max(nia * ni, nja * nj)
    vmem = pl.BlockSpec(memory_space=pltpu.VMEM)
    smem = pl.BlockSpec(memory_space=pltpu.SMEM)
    anywhere = pl.BlockSpec(memory_space=pl.ANY)
    tile = (pairs, size, size)
    flops = 2 * 2 * 3 * size**3 * pairs * 2 * norb * ITERS
    return pl.pallas_call(
        functools.partial(kernel, nia, nja, wire),
        out_shape=(
            jax.ShapeDtypeStruct(amplitudes.shape, F32),
            jax.ShapeDtypeStruct(amplitudes.shape, F32),
        ),
        in_specs=[vmem, vmem] + [smem] * 6 + [vmem, smem, smem, anywhere, anywhere],
        out_specs=(vmem, vmem),
        scratch_shapes=[
            pltpu.VMEM((2,) + row_intersection.shape, F32),
            pltpu.VMEM((ITERS, buffers, wire.planes, size, LANES), F32),
            pltpu.VMEM(tile, F32),
            pltpu.VMEM(tile, F32),
            pltpu.VMEM(tile, F32),
            pltpu.VMEM(tile, BF16),
            pltpu.VMEM(tile, BF16),
            pltpu.SMEM((2, max(ni, nj), norb), jnp.int32),
            pltpu.SMEM((2, max(ni, nj), norb), F32),
            pltpu.SemaphoreType.DMA((2,)),
            pltpu.SemaphoreType.DMA((ITERS, number_sends * len(wire.chunks))),
            pltpu.SemaphoreType.DMA((ITERS, buffers * len(wire.chunks))),
        ],
        compiler_params=pltpu.CompilerParams(
            collective_id=0, has_side_effects=True, vmem_limit_bytes=60 * 1024 * 1024
        ),
        cost_estimate=pl.CostEstimate(flops=flops, bytes_accessed=2 * row_intersection.size * 4, transcendentals=0),
        name="pair_residual",
    )(
        amplitudes, integrals, row_tiles, row_coupling, row_counts, column_tiles, column_coupling,
        column_counts, virtual_energy, first_energy, second_energy, row_intersection, column_intersection,
    )


def solution(mesh):
    pair = P(("grp", "ia"), "ja", None, None)
    placed = (
        pair,
        pair,
        P(("grp", "ia"), "ja", None, None, None),
        P(("grp", "ia"), "ja", None, None, None),
        P(("grp", "ia"), None),
        P(("grp", "ia"), None),
        P(("grp", "ia")),
        P(("grp", "ja"), None),
        P(("grp", "ja"), None),
        P(("grp", "ja")),
        P(("grp", "ia"), "ja", None),
        P(("grp", "ia")),
        P(("grp", "ja")),
    )
    return jax.shard_map(
        functools.partial(local, mesh.shape["ia"], mesh.shape["ja"]),
        mesh=mesh,
        in_specs=placed,
        out_specs=(pair, pair),
        check_vma=False,
    )
```

```python
import functools

import jax
import jax.numpy as jnp
from jax import lax
from jax.experimental import pallas as pl
from jax.experimental.pallas import tpu as pltpu
from jax.sharding import PartitionSpec as P

ITERS = 2
LANES = 128
MESH = pl.DeviceIdType.MESH
BF16 = jnp.bfloat16
F32 = jnp.float32


def split(x):
    high = x.astype(BF16)
    return high, (x - high.astype(F32)).astype(BF16)


def dot(a, b, b_side):
    return lax.dot_general(a, b, (((1,), (b_side,)), ((), ())), preferred_element_type=F32)


def product3(a, b_high, b_low, b_side):
    rows = a.shape[0]
    a_high, a_low = split(a)
    both = dot(jnp.concatenate([a_high, a_low], axis=0), b_high, b_side)
    return both[:rows] + both[rows:] + dot(a_high, b_low, b_side)


class Wire:
    def __init__(self, tiles, size):
        self.tiles, self.size = tiles, size
        self.full = size // LANES
        self.rest = size % LANES
        per = LANES // self.rest if self.rest else 1
        cut = per // tiles if per % tiles == 0 else 1
        self.per, self.cut = per, cut if size % (16 * cut) == 0 else 1
        self.piece = size // self.cut
        self.shared = -(-tiles * self.cut // per) if self.rest else 0
        self.low = tiles * self.full * size
        self.rows = self.low + self.shared * self.piece

    def pieces(self, plane):
        every = [(t, c * self.piece) for t in range(self.tiles) for c in range(self.cut)]
        return every[plane * self.per:(plane + 1) * self.per]


def events_of(chunks, nia, nja):
    cores = 2 if nia % 2 == 0 else 1
    places = nia // cores
    every = range(chunks)
    groups = [[("row", "own", 0, c) for c in every] + [("col", "own", 0, c) for c in every]]
    if cores == 2:
        groups += [[("row", "core", 0, c)] for c in every]
    for t in range(1, max(places, nja)):
        for c in every:
            if t < nja:
                groups.append([("col", "up", t, c), ("col", "down", t, c)])
            if t < places:
                groups.append([("row", "place", t, c)])
        if t < places and cores == 2:
            groups += [[("row", "core", t, c)] for c in every]
    return cores, places, groups


def buffers_of(cores, places, nja):
    keys = [("own", 0)] + [("core", t) for t in range(places) if cores == 2]
    keys += [("place", t) for t in range(1, places)]
    keys += [(how, t) for how in ("up", "down") for t in range(1, nja)]
    return {key: number for number, key in enumerate(keys)}


def kernel(
    nia, nja, wire,
    row_tiles, row_coup, row_counts, col_tiles, col_coup, col_counts, virt, first, second,
    amp, integ, row_s, col_s,
    cur, acc,
    s_all, buf, given, den, t_high, t_low, slot_tab, weight_tab, load_sem, send_sem, recv_sem,
):
    ni, nj, size, _ = amp.shape
    slots = row_tiles.shape[1]
    cores, places, groups = events_of(ni, nia, nja)
    where = buffers_of(cores, places, nja)
    me_a, me_z = lax.axis_index("ia"), lax.axis_index("ja")
    place, core = me_a // cores, me_a % cores
    norbs = (nia * ni, nja * nj)

    loads = [
        pltpu.make_async_copy(amp, cur, load_sem.at[0]),
        pltpu.make_async_copy(row_s, s_all.at[0], load_sem.at[1]),
        pltpu.make_async_copy(col_s, s_all.at[1], load_sem.at[2]),
        pltpu.make_async_copy(integ, given, load_sem.at[3]),
    ]
    for load in loads:
        load.start()

    def sibling():
        return {"ia": place * cores + (core + 1) % cores}

    def placed(step):
        return {"ia": ((place + step) % places) * cores + core}

    has_up, has_down = me_z < nja - 1, me_z > 0

    barrier = pltpu.get_barrier_semaphore()

    def greet(device):
        pl.semaphore_signal(barrier, inc=1, device_id=device, device_id_type=MESH)

    if cores == 2:
        greet(sibling())
    for step in range(1, places):
        greet(placed(step))
    if nja > 1:
        @pl.when(has_up)
        def _():
            greet({"ja": me_z + 1})

        @pl.when(has_down)
        def _():
            greet({"ja": me_z - 1})

    def here_of(how, step):
        if how == "up":
            return me_z - step >= 0
        if how == "down":
            return me_z + step < nja
        return None

    def source_of(kind, how, step):
        if kind == "col":
            return {"up": me_z - step, "down": me_z + step, "own": me_z}[how]
        flip = 1 if how == "core" else 0
        return ((place + places - step) % places) * cores + (core + flip) % cores

    sends = []
    for t in range(0, nja - 1):
        before = (lambda how: (how, t) if t else ("own", 0))
        sends.append((before("up"), ("up", t + 1), {"ja": me_z + 1}, has_up & (me_z - t >= 0)))
        sends.append((before("down"), ("down", t + 1), {"ja": me_z - 1}, has_down & (me_z + t < nja)))
    for t in range(1, places):
        sends.append((("own", 0), ("place", t), placed(t), None))
    if cores == 2:
        for t in range(places):
            sends.append((("place", t) if t else ("own", 0), ("core", t), sibling(), None))

    def copy(it, chunk, number, here, there, device):
        return pltpu.make_async_remote_copy(
            src_ref=buf.at[it, where[here], chunk],
            dst_ref=buf.at[it, where[there], chunk],
            send_sem=send_sem.at[it, number, chunk],
            recv_sem=recv_sem.at[it, where[there], chunk],
            device_id=device,
            device_id_type=MESH,
        )

    def guarded(condition, act):
        if condition is None:
            act()
        else:
            pl.when(condition)(act)

    def send_after(key, it, chunk):
        for number, (here, there, device, condition) in enumerate(sends):
            if here == key:
                guarded(condition, lambda: copy(it, chunk, number, here, there, device).start())

    def take(key, it, chunk):
        copy(it, chunk, 0, key, key, {"ja": me_z, "ia": me_a}).wait_recv()
        send_after(key, it, chunk)

    def send_own(it, c):
        for t in range(nj):
            for f in range(wire.full):
                row = (t * wire.full + f) * size
                buf[it, 0, c, row:row + size] = cur[c, t, :, f * LANES:(f + 1) * LANES]
        for plane in range(wire.shared):
            some = [
                cur[c, t, row:row + wire.piece, wire.full * LANES:] for t, row in wire.pieces(plane)
            ]
            room = LANES - len(some) * wire.rest
            if room:
                some.append(jnp.zeros((wire.piece, room), F32))
            row = wire.low + plane * wire.piece
            buf[it, 0, c, row:row + wire.piece] = jnp.concatenate(some, axis=1)
        send_after(("own", 0), it, c)

    greeted = (1 if cores == 2 else 0) + places - 1
    if nja > 1:
        greeted = greeted + has_up.astype(jnp.int32) + has_down.astype(jnp.int32)
    loads[0].wait()
    pl.semaphore_wait(barrier, greeted)
    for c in range(ni):
        send_own(0, c)

    for kind, (tiles, coup, counts, count) in enumerate(
        ((row_tiles, row_coup, row_counts, ni), (col_tiles, col_coup, col_counts, nj))
    ):
        for a in range(count):
            def fill(k, carry, kind=kind, tiles=tiles, coup=coup, counts=counts, a=a):
                slot, weight = jnp.int32(0), F32(0)
                live = counts[a]
                for l in range(slots):
                    match = tiles[a, l] == k
                    slot = jnp.where(match, jnp.int32(l), slot)
                    weight = jnp.where(match & (l < live), coup[a, l], weight)
                slot_tab[kind, a, k] = slot
                weight_tab[kind, a, k] = weight
                return carry

            lax.fori_loop(0, norbs[kind], fill, 0)

    rows_of = lax.broadcasted_iota(jnp.int32, (size, size), 0)
    columns_of = lax.broadcasted_iota(jnp.int32, (size, size), 1)
    for i in range(ni):
        for j in range(nj):
            across = virt[i, j:j + 1, :]
            down = jnp.sum(jnp.where(rows_of == columns_of, across, 0.0), axis=1, keepdims=True)
            den[i, j] = down + across - first[i] - second[j]
            acc[i, j] = jnp.zeros((size, size), F32)

    for load in loads[1:]:
        load.wait()

    flat = [event for group in groups for event in group]

    def pick(e, values):
        out = values[0]
        for index in range(1, len(values)):
            if values[index] is not values[index - 1]:
                out = jnp.where(e >= index, values[index], out)
        return out

    def one_event(it, e):
        start = 0
        for group in groups:
            def take_group(group=group):
                for kind, how, step, chunk in group:
                    guarded(here_of(how, step), lambda: take((how, step), it, chunk))

            if group[0][1] != "own":
                pl.when(e == start)(take_group)
            start += len(group)

        kind = pick(e, [jnp.int32(event[0] == "col") for event in flat])
        index = pick(e, [jnp.int32(where[event[1], event[2]]) for event in flat])
        chunk = pick(e, [jnp.int32(event[3]) for event in flat])
        source = pick(e, [source_of(*event[:3]) for event in flat])
        present = [here_of(event[1], event[2]) for event in flat]
        here = pick(e, [jnp.int32(1) if x is None else x.astype(jnp.int32) for x in present]) > 0

        @pl.when(here)
        def _():
            for t in range(nj):
                for f in range(wire.full):
                    lanes = slice(f * LANES, (f + 1) * LANES)
                    row = (t * wire.full + f) * size
                    t_high[t, :, lanes], t_low[t, :, lanes] = split(buf[it, index, chunk, row:row + size])
            for plane in range(wire.shared):
                low = wire.low + plane * wire.piece
                part = buf[it, index, chunk, low:low + wire.piece]
                for q, (t, row) in enumerate(wire.pieces(plane)):
                    mine = pltpu.roll(part, LANES - q * wire.rest, 1) if q else part
                    high, low_part = split(mine[:, :wire.rest])
                    t_high[t, row:row + wire.piece, wire.full * LANES:] = high
                    t_low[t, row:row + wire.piece, wire.full * LANES:] = low_part

            is_row = kind == 0

            def products(a):
                orbital = jnp.where(is_row, source * ni + chunk, source * nj + a)
                i = jnp.where(is_row, a, chunk)
                out = []
                for j in range(nj):
                    mine = jnp.where(is_row, a, j)
                    tile = jnp.where(is_row, j, a)
                    slot = slot_tab[kind, mine, orbital]
                    weight = weight_tab[kind, mine, orbital]
                    s_high, s_low = split(s_all[kind, i, j, slot])
                    x = dot(jnp.concatenate([s_high, s_low], axis=0), t_high[tile], 0)
                    x = x[:size] + x[size:] + dot(s_high, t_low[tile], 0)
                    out.append((i, j, x * weight, s_high, s_low))
                return out

            def finish(out):
                for i, j, x, s_high, s_low in out:
                    acc[i, j] += product3(x, s_high, s_low, 1)

            if ni == nj:
                some = [products(a) for a in range(ni)]
                for out in some:
                    finish(out)
            else:
                def one(a, carry):
                    finish(products(a))
                    return carry

                lax.fori_loop(0, jnp.where(is_row, ni, nj), one, 0)

    def one_iteration(it, carry):
        def step(e, inner):
            one_event(it, e)
            return inner

        lax.fori_loop(0, len(flat), step, 0)

        @pl.when(it < ITERS - 1)
        def _():
            for i in range(ni):
                for j in range(nj):
                    residual = given[i, j] + den[i, j] * cur[i, j] - acc[i, j]
                    cur[i, j] = cur[i, j] - residual / den[i, j]
                    acc[i, j] = jnp.zeros((size, size), F32)
                send_own(it + 1, i)

        return carry

    lax.fori_loop(0, ITERS, one_iteration, 0)

    def drain(it, carry):
        for number, (here, there, device, condition) in enumerate(sends):
            for chunk in range(ni):
                guarded(condition, lambda: copy(it, chunk, number, here, there, device).wait_send())
        return carry

    lax.fori_loop(0, ITERS, drain, 0)


def local(
    nia, nja,
    amplitudes, integrals, row_intersection, column_intersection, row_tiles, row_coupling, row_counts,
    column_tiles, column_coupling, column_counts, virtual_energy, first_energy, second_energy,
):
    ni, nj, size, _ = amplitudes.shape
    wire = Wire(nj, size)
    cores, places, groups = events_of(ni, nia, nja)
    buffers = len(buffers_of(cores, places, nja))
    number_sends = 2 * (nja - 1) + (places - 1) + (places if cores == 2 else 0)
    norb = max(nia * ni, nja * nj)
    vmem = pl.BlockSpec(memory_space=pltpu.VMEM)
    smem = pl.BlockSpec(memory_space=pltpu.SMEM)
    anywhere = pl.BlockSpec(memory_space=pl.ANY)
    flops = 2 * 2 * 3 * size**3 * ni * nj * 2 * norb * ITERS
    shape = jax.ShapeDtypeStruct(amplitudes.shape, F32)
    current, terms = pl.pallas_call(
        functools.partial(kernel, nia, nja, wire),
        out_shape=(shape, shape),
        in_specs=[smem] * 6 + [vmem, smem, smem] + [anywhere] * 4,
        out_specs=(vmem, vmem),
        scratch_shapes=[
            pltpu.VMEM((2,) + row_intersection.shape, F32),
            pltpu.VMEM((ITERS, buffers, ni, wire.rows, LANES), F32),
            pltpu.VMEM(amplitudes.shape, F32),
            pltpu.VMEM(amplitudes.shape, F32),
            pltpu.VMEM((nj, size, size), BF16),
            pltpu.VMEM((nj, size, size), BF16),
            pltpu.SMEM((2, max(ni, nj), norb), jnp.int32),
            pltpu.SMEM((2, max(ni, nj), norb), F32),
            pltpu.SemaphoreType.DMA((4,)),
            pltpu.SemaphoreType.DMA((ITERS, max(number_sends, 1), ni)),
            pltpu.SemaphoreType.DMA((ITERS, buffers, ni)),
        ],
        compiler_params=pltpu.CompilerParams(
            collective_id=0, has_side_effects=True, vmem_limit_bytes=60 * 1024 * 1024
        ),
        cost_estimate=pl.CostEstimate(flops=flops, bytes_accessed=2 * row_intersection.size * 4, transcendentals=0),
        name="pair_residual",
    )(
        row_tiles, row_coupling, row_counts, column_tiles, column_coupling, column_counts, virtual_energy,
        first_energy, second_energy, amplitudes, integrals, row_intersection, column_intersection,
    )
    denom = (
        virtual_energy[:, :, :, None]
        + virtual_energy[:, :, None, :]
        - first_energy[:, None, None, None]
        - second_energy[None, :, None, None]
    )
    residual = integrals + denom * current - terms
    return current - residual / denom, residual


def solution(mesh):
    pair = P(("grp", "ia"), "ja", None, None)
    placed = (
        pair,
        pair,
        P(("grp", "ia"), "ja", None, None, None),
        P(("grp", "ia"), "ja", None, None, None),
        P(("grp", "ia"), None),
        P(("grp", "ia"), None),
        P(("grp", "ia")),
        P(("grp", "ja"), None),
        P(("grp", "ja"), None),
        P(("grp", "ja")),
        P(("grp", "ia"), "ja", None),
        P(("grp", "ia")),
        P(("grp", "ja")),
    )
    return jax.shard_map(
        functools.partial(local, mesh.shape["ia"], mesh.shape["ja"]),
        mesh=mesh,
        in_specs=placed,
        out_specs=(pair, pair),
        check_vma=False,
    )
```

```python
import functools

import jax
import jax.numpy as jnp
from jax import lax
from jax.experimental import pallas as pl
from jax.experimental.pallas import tpu as pltpu
from jax.sharding import PartitionSpec as P

ITERS = 2
LANES = 128
MESH = pl.DeviceIdType.MESH
BF16 = jnp.bfloat16
F32 = jnp.float32


def split(x):
    high = x.astype(BF16)
    return high, (x - high.astype(F32)).astype(BF16)


def dot(a, b, b_side):
    return lax.dot_general(a, b, (((1,), (b_side,)), ((), ())), preferred_element_type=F32)


def product3(a, b_high, b_low, b_side):
    rows = a.shape[0]
    a_high, a_low = split(a)
    both = dot(jnp.concatenate([a_high, a_low], axis=0), b_high, b_side)
    return both[:rows] + both[rows:] + dot(a_high, b_low, b_side)


class Wire:
    def __init__(self, tiles, size):
        self.tiles, self.size = tiles, size
        self.full = size // LANES
        self.rest = size % LANES
        per = LANES // self.rest if self.rest else 1
        cut = per // tiles if per % tiles == 0 else 1
        self.per, self.cut = per, cut if size % (16 * cut) == 0 else 1
        self.piece = size // self.cut
        self.shared = -(-tiles * self.cut // per) if self.rest else 0
        self.low = tiles * self.full * size
        self.rows = self.low + self.shared * self.piece

    def pieces(self, plane):
        every = [(t, c * self.piece) for t in range(self.tiles) for c in range(self.cut)]
        return every[plane * self.per:(plane + 1) * self.per]


def events_of(chunks, nia, nja):
    cores = 2 if nia % 2 == 0 else 1
    places = nia // cores
    every = range(chunks)
    groups = [[("row", "own", 0, c) for c in every] + [("col", "own", 0, c) for c in every]]
    if cores == 2:
        groups += [[("row", "core", 0, c)] for c in every]
    for t in range(1, max(places, nja)):
        for c in every:
            if t < nja:
                groups.append([("col", "up", t, c), ("col", "down", t, c)])
            if t < places:
                groups.append([("row", "place", t, c)])
        if t < places and cores == 2:
            groups += [[("row", "core", t, c)] for c in every]
    return cores, places, groups


def buffers_of(cores, places, nja):
    keys = [("own", 0)] + [("core", t) for t in range(places) if cores == 2]
    keys += [("place", t) for t in range(1, places)]
    keys += [(how, t) for how in ("up", "down") for t in range(1, nja)]
    return {key: number for number, key in enumerate(keys)}


def kernel(
    nia, nja, wire,
    row_tiles, row_coup, row_counts, col_tiles, col_coup, col_counts, virt, first, second,
    amp, integ, row_s, col_s,
    cur, acc,
    s_all, buf, given, den, t_high, t_low, slot_tab, weight_tab, load_sem, send_sem, recv_sem,
):
    ni, nj, size, _ = amp.shape
    slots = row_tiles.shape[1]
    cores, places, groups = events_of(ni, nia, nja)
    where = buffers_of(cores, places, nja)
    me_a, me_z = lax.axis_index("ia"), lax.axis_index("ja")
    place, core = me_a // cores, me_a % cores
    norbs = (nia * ni, nja * nj)

    loads = [
        pltpu.make_async_copy(amp, cur, load_sem.at[0]),
        pltpu.make_async_copy(row_s, s_all.at[0], load_sem.at[1]),
        pltpu.make_async_copy(col_s, s_all.at[1], load_sem.at[2]),
        pltpu.make_async_copy(integ, given, load_sem.at[3]),
    ]
    for load in loads:
        load.start()

    def sibling():
        return {"ia": place * cores + (core + 1) % cores}

    def placed(step):
        return {"ia": ((place + step) % places) * cores + core}

    has_up, has_down = me_z < nja - 1, me_z > 0

    barrier = pltpu.get_barrier_semaphore()

    def greet(device):
        pl.semaphore_signal(barrier, inc=1, device_id=device, device_id_type=MESH)

    if cores == 2:
        greet(sibling())
    for step in range(1, places):
        greet(placed(step))
    if nja > 1:
        @pl.when(has_up)
        def _():
            greet({"ja": me_z + 1})

        @pl.when(has_down)
        def _():
            greet({"ja": me_z - 1})

    def here_of(how, step):
        if how == "up":
            return me_z - step >= 0
        if how == "down":
            return me_z + step < nja
        return None

    def source_of(kind, how, step):
        if kind == "col":
            return {"up": me_z - step, "down": me_z + step, "own": me_z}[how]
        flip = 1 if how == "core" else 0
        return ((place + places - step) % places) * cores + (core + flip) % cores

    sends = []
    for t in range(0, nja - 1):
        before = (lambda how: (how, t) if t else ("own", 0))
        sends.append((before("up"), ("up", t + 1), {"ja": me_z + 1}, has_up & (me_z - t >= 0)))
        sends.append((before("down"), ("down", t + 1), {"ja": me_z - 1}, has_down & (me_z + t < nja)))
    for t in range(1, places):
        sends.append((("own", 0), ("place", t), placed(t), None))
    if cores == 2:
        for t in range(places):
            sends.append((("place", t) if t else ("own", 0), ("core", t), sibling(), None))

    def copy(it, chunk, number, here, there, device):
        return pltpu.make_async_remote_copy(
            src_ref=buf.at[it, where[here], chunk],
            dst_ref=buf.at[it, where[there], chunk],
            send_sem=send_sem.at[it, number, chunk],
            recv_sem=recv_sem.at[it, where[there], chunk],
            device_id=device,
            device_id_type=MESH,
        )

    def guarded(condition, act):
        if condition is None:
            act()
        else:
            pl.when(condition)(act)

    def send_after(key, it, chunk):
        for number, (here, there, device, condition) in enumerate(sends):
            if here == key:
                guarded(condition, lambda: copy(it, chunk, number, here, there, device).start())

    def take(key, it, chunk):
        copy(it, chunk, 0, key, key, {"ja": me_z, "ia": me_a}).wait_recv()
        send_after(key, it, chunk)

    def send_own(it, c):
        for t in range(nj):
            for f in range(wire.full):
                row = (t * wire.full + f) * size
                buf[it, 0, c, row:row + size] = cur[c, t, :, f * LANES:(f + 1) * LANES]
        for plane in range(wire.shared):
            some = [
                cur[c, t, row:row + wire.piece, wire.full * LANES:] for t, row in wire.pieces(plane)
            ]
            room = LANES - len(some) * wire.rest
            if room:
                some.append(jnp.zeros((wire.piece, room), F32))
            row = wire.low + plane * wire.piece
            buf[it, 0, c, row:row + wire.piece] = jnp.concatenate(some, axis=1)
        send_after(("own", 0), it, c)

    greeted = (1 if cores == 2 else 0) + places - 1
    if nja > 1:
        greeted = greeted + has_up.astype(jnp.int32) + has_down.astype(jnp.int32)
    loads[0].wait()
    pl.semaphore_wait(barrier, greeted)
    for c in range(ni):
        send_own(0, c)

    for kind, (tiles, coup, counts, count) in enumerate(
        ((row_tiles, row_coup, row_counts, ni), (col_tiles, col_coup, col_counts, nj))
    ):
        for a in range(count):
            def fill(k, carry, kind=kind, tiles=tiles, coup=coup, counts=counts, a=a):
                slot, weight = jnp.int32(0), F32(0)
                live = counts[a]
                for l in range(slots):
                    match = tiles[a, l] == k
                    slot = jnp.where(match, jnp.int32(l), slot)
                    weight = jnp.where(match & (l < live), coup[a, l], weight)
                slot_tab[kind, a, k] = slot
                weight_tab[kind, a, k] = weight
                return carry

            lax.fori_loop(0, norbs[kind], fill, 0)

    rows_of = lax.broadcasted_iota(jnp.int32, (size, size), 0)
    columns_of = lax.broadcasted_iota(jnp.int32, (size, size), 1)
    for i in range(ni):
        for j in range(nj):
            across = virt[i, j:j + 1, :]
            down = jnp.sum(jnp.where(rows_of == columns_of, across, 0.0), axis=1, keepdims=True)
            den[i, j] = down + across - first[i] - second[j]
            acc[i, j] = jnp.zeros((size, size), F32)

    for load in loads[1:]:
        load.wait()

    flat = [event for group in groups for event in group]

    def pick(e, values):
        out = values[0]
        for index in range(1, len(values)):
            if values[index] is not values[index - 1]:
                out = jnp.where(e >= index, values[index], out)
        return out

    def one_event(it, e):
        start = 0
        for group in groups:
            def take_group(group=group):
                for kind, how, step, chunk in group:
                    guarded(here_of(how, step), lambda: take((how, step), it, chunk))

            if group[0][1] != "own":
                pl.when(e == start)(take_group)
            start += len(group)

        kind = pick(e, [jnp.int32(event[0] == "col") for event in flat])
        index = pick(e, [jnp.int32(where[event[1], event[2]]) for event in flat])
        chunk = pick(e, [jnp.int32(event[3]) for event in flat])
        source = pick(e, [source_of(*event[:3]) for event in flat])
        present = [here_of(event[1], event[2]) for event in flat]
        here = pick(e, [jnp.int32(1) if x is None else x.astype(jnp.int32) for x in present]) > 0

        @pl.when(here)
        def _():
            for t in range(nj):
                for f in range(wire.full):
                    lanes = slice(f * LANES, (f + 1) * LANES)
                    row = (t * wire.full + f) * size
                    t_high[t, :, lanes], t_low[t, :, lanes] = split(buf[it, index, chunk, row:row + size])
            for plane in range(wire.shared):
                low = wire.low + plane * wire.piece
                part = buf[it, index, chunk, low:low + wire.piece]
                for q, (t, row) in enumerate(wire.pieces(plane)):
                    mine = pltpu.roll(part, LANES - q * wire.rest, 1) if q else part
                    high, low_part = split(mine[:, :wire.rest])
                    t_high[t, row:row + wire.piece, wire.full * LANES:] = high
                    t_low[t, row:row + wire.piece, wire.full * LANES:] = low_part

            is_row = kind == 0

            def products(a):
                orbital = jnp.where(is_row, source * ni + chunk, source * nj + a)
                i = jnp.where(is_row, a, chunk)
                out = []
                for j in range(nj):
                    mine = jnp.where(is_row, a, j)
                    tile = jnp.where(is_row, j, a)
                    slot = slot_tab[kind, mine, orbital]
                    weight = weight_tab[kind, mine, orbital]
                    s_high, s_low = split(s_all[kind, i, j, slot])
                    x = dot(jnp.concatenate([s_high, s_low], axis=0), t_high[tile], 0)
                    x = x[:size] + x[size:] + dot(s_high, t_low[tile], 0)
                    out.append((i, j, x * weight, s_high, s_low))
                return out

            def finish(out):
                for i, j, x, s_high, s_low in out:
                    acc[i, j] += product3(x, s_high, s_low, 1)

            if ni == nj:
                some = [products(a) for a in range(ni)]
                for out in some:
                    finish(out)
            else:
                def one(a, carry):
                    finish(products(a))
                    return carry

                lax.fori_loop(0, jnp.where(is_row, ni, nj), one, 0)

    def one_iteration(it, carry):
        def step(e, inner):
            one_event(it, e)
            return inner

        lax.fori_loop(0, len(flat), step, 0)

        @pl.when(it < ITERS - 1)
        def _():
            for i in range(ni):
                for j in range(nj):
                    residual = given[i, j] + den[i, j] * cur[i, j] - acc[i, j]
                    cur[i, j] = cur[i, j] - residual / den[i, j]
                    acc[i, j] = jnp.zeros((size, size), F32)
                send_own(it + 1, i)

        return carry

    lax.fori_loop(0, ITERS, one_iteration, 0)

    def drain(it, carry):
        for number, (here, there, device, condition) in enumerate(sends):
            for chunk in range(ni):
                guarded(condition, lambda: copy(it, chunk, number, here, there, device).wait_send())
        return carry

    lax.fori_loop(0, ITERS, drain, 0)


def local(
    nia, nja,
    amplitudes, integrals, row_intersection, column_intersection, row_tiles, row_coupling, row_counts,
    column_tiles, column_coupling, column_counts, virtual_energy, first_energy, second_energy,
):
    ni, nj, size, _ = amplitudes.shape
    wire = Wire(nj, size)
    cores, places, groups = events_of(ni, nia, nja)
    buffers = len(buffers_of(cores, places, nja))
    number_sends = 2 * (nja - 1) + (places - 1) + (places if cores == 2 else 0)
    norb = max(nia * ni, nja * nj)
    vmem = pl.BlockSpec(memory_space=pltpu.VMEM)
    smem = pl.BlockSpec(memory_space=pltpu.SMEM)
    anywhere = pl.BlockSpec(memory_space=pl.ANY)
    flops = 2 * 2 * 3 * size**3 * ni * nj * 2 * norb * ITERS
    shape = pltpu.VMEM(amplitudes.shape, F32)
    current, terms = pl.pallas_call(
        functools.partial(kernel, nia, nja, wire),
        out_shape=(shape, shape),
        in_specs=[smem] * 6 + [vmem, smem, smem] + [anywhere] * 4,
        out_specs=(vmem, vmem),
        scratch_shapes=[
            pltpu.VMEM((2,) + row_intersection.shape, F32),
            pltpu.VMEM((ITERS, buffers, ni, wire.rows, LANES), F32),
            pltpu.VMEM(amplitudes.shape, F32),
            pltpu.VMEM(amplitudes.shape, F32),
            pltpu.VMEM((nj, size, size), BF16),
            pltpu.VMEM((nj, size, size), BF16),
            pltpu.SMEM((2, max(ni, nj), norb), jnp.int32),
            pltpu.SMEM((2, max(ni, nj), norb), F32),
            pltpu.SemaphoreType.DMA((4,)),
            pltpu.SemaphoreType.DMA((ITERS, max(number_sends, 1), ni)),
            pltpu.SemaphoreType.DMA((ITERS, buffers, ni)),
        ],
        compiler_params=pltpu.CompilerParams(
            collective_id=0, has_side_effects=True, vmem_limit_bytes=60 * 1024 * 1024
        ),
        cost_estimate=pl.CostEstimate(flops=flops, bytes_accessed=2 * row_intersection.size * 4, transcendentals=0),
        name="pair_residual",
    )(
        row_tiles, row_coupling, row_counts, column_tiles, column_coupling, column_counts, virtual_energy,
        first_energy, second_energy, amplitudes, integrals, row_intersection, column_intersection,
    )
    denom = (
        virtual_energy[:, :, :, None]
        + virtual_energy[:, :, None, :]
        - first_energy[:, None, None, None]
        - second_energy[None, :, None, None]
    )
    residual = integrals + denom * current - terms
    return current - residual / denom, residual


def solution(mesh):
    pair = P(("grp", "ia"), "ja", None, None)
    placed = (
        pair,
        pair,
        P(("grp", "ia"), "ja", None, None, None),
        P(("grp", "ia"), "ja", None, None, None),
        P(("grp", "ia"), None),
        P(("grp", "ia"), None),
        P(("grp", "ia")),
        P(("grp", "ja"), None),
        P(("grp", "ja"), None),
        P(("grp", "ja")),
        P(("grp", "ia"), "ja", None),
        P(("grp", "ia")),
        P(("grp", "ja")),
    )
    return jax.shard_map(
        functools.partial(local, mesh.shape["ia"], mesh.shape["ja"]),
        mesh=mesh,
        in_specs=placed,
        out_specs=(pair, pair),
        check_vma=False,
    )
```
